32 devices in a mesh: doc: 4 (over y, x), label: 8 (over z, core).
Axes of the slice: x: 2, y: 2, z: 4, core: 2. Of those that a mesh axis runs over, the one named last changes fastest.
Arguments:
- doc_embed: bfloat16 [1024, 768], P(('doc', 'label')), may hold values from -0.59765625 to 0.59765625
- classifier: bfloat16 [8192, 768], P('label'), may hold values from -4.28125 to 4.28125
- centroids: bfloat16 [64, 768], P('doc'), may hold values from -4.28125 to 4.28125
- shortlist: int32 [1024, 32], P(('doc', 'label')), may hold values from 0 to 63, all different within a row
- positives: int32 [1024, 4], P(('doc', 'label')), may hold values from 0 to 4095
Outputs:
- grad_classifier: bfloat16 [8192, 768], P('label')
- grad_centroids: float32 [64, 768], P('doc')
- grad_docs: bfloat16 [1024, 768], P(('doc', 'label'))
The draws below stay inside these ranges and needn't reach their ends.
Inputs may be any that keep to these rules, and one draw needn't show every extreme that they name: `shortlist`: each row names 32 different clusters; every cluster is named by some row.
All inputs are finite; a program needn't handle non-finite values.
Results may differ from the reference program's by a relative error of at most 0.015.
Values may be sent and summed in bfloat16 or wider, within the bound.
A program may use at most 64 MiB of HBM per device.

```python
import jax
import jax.numpy as jnp
from jax import lax

D = 768
CLS = 128
CL_LAB = 8
DOC_DEV = 32
SHORT = 32
POS = 4
CLUSTERS = 64
LABELS = 8192
DOCS = 1024
N_DOC = 4
N_LABEL = 8


def set_ends(entries, rng, low, top_value):
    extent = entries.shape
    place = [jax.random.randint(jax.random.fold_in(rng, axis), (), 0, extent[axis]) for axis in range(len(extent))]
    entries = entries.at[tuple(place)].set(low)
    longest = extent.index(max(extent))
    place[longest] = (place[longest] + 1) % extent[longest]
    return entries.at[tuple(place)].set(top_value)


def level_of(own_key, dims, cuts, least, high):
    def one(axis_at, blocks):
        draws = jax.random.uniform(jax.random.fold_in(jax.random.fold_in(own_key, 6), axis_at), (blocks,), jnp.float32, least / len(cuts), high / len(cuts))
        return jnp.repeat(jnp.exp(draws), dims[axis_at] // blocks).reshape((-1,) + (1,) * (len(dims) - axis_at - 1))

    loudness = one(*cuts[0])
    for cut in cuts[1:]:
        loudness = loudness * one(*cut)
    return loudness


def picks_of(stream_key, rows, amount, top, lift):
    ranking = jax.random.permutation(jax.random.fold_in(stream_key, 1), amount)
    favour = ranking
    for power in range(3):
        favour = favour * favour // amount
    favour = favour * lift // amount
    tickets = jax.random.randint(jax.random.fold_in(stream_key, 2), (rows, amount), 0, 4096) + favour
    sure = jax.random.permutation(jax.random.fold_in(stream_key, 3), rows)[jnp.arange(amount) % rows]
    tickets = jnp.where(jnp.arange(rows)[:, None] == sure[None, :], 1 << 14, tickets)
    merit = tickets * amount + jnp.arange(amount)
    return lax.top_k(merit.astype(jnp.int32), top)[1].astype(jnp.int32)


def noise(stream_key, dims, spread, most, split=(), held_as=jnp.bfloat16):
    drawn = spread * jax.random.normal(stream_key, dims, jnp.float32)
    if split:
        drawn = drawn * level_of(stream_key, dims, split, -0.22, 0.18)
    return jnp.clip(drawn, -most, most).astype(held_as)


def setup_inputs(seed: int = 0) -> dict:
    splits = jax.random.split(jax.random.key(seed), 6)
    doc_embed = noise(splits[0], (DOCS, D), 0.1, 0.59765625, ((0, 32),))
    classifier = noise(splits[1], (LABELS, D), 0.72, 4.28125, ((0, 8),))
    centroids = noise(splits[2], (CLUSTERS, D), 0.72, 4.28125, ((0, 4),))
    shortlist = picks_of(splits[3], DOCS, CLUSTERS, SHORT, 8192)
    positives = set_ends(jax.random.randint(splits[4], (DOCS, POS), 0, SHORT * CLS), jax.random.fold_in(splits[4], 1), 0, (SHORT * CLS) - 1).astype(jnp.int32)
    return dict(doc_embed=doc_embed, classifier=classifier, centroids=centroids, shortlist=shortlist, positives=positives)


LOSS_WEIGHT = 0.125


def reference(doc_embed, classifier, centroids, shortlist, positives):
    pos_cluster = jnp.take_along_axis(shortlist, (positives // CLS).astype(jnp.int32), axis=1)
    pos_label = pos_cluster * CLS + positives % CLS
    cluster_ids = jnp.arange(CLUSTERS, dtype=jnp.int32)
    label_ids = jnp.arange(LABELS, dtype=jnp.int32)
    group = DOC_DEV * N_LABEL
    labels_dev = CL_LAB * CLS
    weights_blocks = classifier.astype(jnp.float32).reshape(N_LABEL, labels_dev, D)
    cent_blocks = centroids.astype(jnp.float32).reshape(N_LABEL, CL_LAB, D)

    def one_group(carry, index):
        class_sum, cent_sum = carry
        start = (index * group).astype(jnp.int32)
        rows = lax.dynamic_slice_in_dim(doc_embed, start, group, 0)
        short_rows = lax.dynamic_slice_in_dim(shortlist, start, group, 0)
        pos_rows = lax.dynamic_slice_in_dim(pos_label, start, group, 0)
        pcl_rows = lax.dynamic_slice_in_dim(pos_cluster, start, group, 0)
        meta_logits = jnp.dot(rows, centroids.T, preferred_element_type=jnp.float32)
        meta_target = jnp.any(pcl_rows[:, :, None] == cluster_ids[None, None, :], axis=1)
        meta_grad = (LOSS_WEIGHT * (jax.nn.sigmoid(meta_logits) - meta_target.astype(jnp.float32))).astype(jnp.bfloat16)
        cent_part = jnp.dot(meta_grad.T, rows, preferred_element_type=jnp.float32)
        logits = jnp.dot(rows, classifier.T, preferred_element_type=jnp.float32)
        member = jnp.any(short_rows[:, :, None] == cluster_ids[None, None, :], axis=1)
        mask = jnp.repeat(member, CLS, axis=1)
        target = jnp.any(pos_rows[:, :, None] == label_ids[None, None, :], axis=1)
        grad = (LOSS_WEIGHT * (jax.nn.sigmoid(logits) - target.astype(jnp.float32)) * mask.astype(jnp.float32)).astype(jnp.bfloat16)
        class_part = jnp.dot(grad.T, rows, preferred_element_type=jnp.float32).astype(jnp.bfloat16)
        parts = jnp.einsum("nla,lad->lnd", grad.astype(jnp.float32).reshape(group, N_LABEL, labels_dev), weights_blocks)
        parts = parts + jnp.einsum("nlc,lcd->lnd", meta_grad.astype(jnp.float32).reshape(group, N_LABEL, CL_LAB), cent_blocks)
        input_sum = jnp.sum(parts.astype(jnp.bfloat16).astype(jnp.float32), axis=0)
        return (class_sum + class_part.astype(jnp.float32), cent_sum + cent_part), input_sum

    start_carry = (jnp.zeros((LABELS, D), jnp.float32), jnp.zeros((CLUSTERS, D), jnp.float32))
    sums, inputs = lax.scan(one_group, start_carry, jnp.arange(N_DOC, dtype=jnp.int32))
    grad_docs = inputs.reshape(DOCS, D).astype(jnp.bfloat16)
    return sums[0].astype(jnp.bfloat16), sums[1], grad_docs
```

```python
import functools

import jax
import jax.numpy as jnp
from jax import lax
from jax.experimental import pallas as pl
from jax.experimental.pallas import tpu as pltpu
from jax.sharding import PartitionSpec as P

CLS = 128
INFO = 128
TILE = 256
EIGHTH = 0.125
F32 = jnp.float32
BF16 = jnp.bfloat16
MESH = pl.DeviceIdType.MESH
NT = (((1,), (1,)), ((), ()))
TN = (((0,), (0,)), ((), ()))


def flip(a, k, n):
    out, bit = 0, 1
    while bit < n:
        b = lax.rem(lax.div(a, bit), 2)
        out = out + bit * ((1 - b) if (k // bit) % 2 else b)
        bit *= 2
    return out


def sigmoid_grad(logits, target):
    return (EIGHTH / 2) * jnp.tanh(0.5 * logits) + jnp.where(target, -EIGHTH / 2, EIGHTH / 2)


def kernel(
    n_doc, n_label, pos_n,
    doc_ref, cls_hbm, cent_ref, short_ref, pos_ref,
    gcls_ref, gcent_ref, gdoc_ref,
    docs, cls, info_t, acc, part, cent_in, pair_out, pair_in, tot, rs_out, rs_in,
    cls_sem, sib_send, z_send, g_send, cent_send, pair_send, rs_send,
    recv, cent_recv, pair_recv, rs_recv,
):
    rows, width = doc_ref.shape
    labels = cls.shape[0]
    here = labels // CLS
    per = cent_ref.shape[0]
    n_z = n_label // 2
    group = n_label * rows
    d = lax.axis_index("doc")
    l = lax.axis_index("label")
    z, c = lax.div(l, 2), lax.rem(l, 2)
    sib = z * 2 + (1 - c)

    load = pltpu.make_async_copy(cls_hbm, cls, cls_sem)
    load.start()

    barrier = pltpu.get_barrier_semaphore()
    peers = [(d, sib)]
    peers += [(d, flip(z, k, n_z) * 2 + c) for k in range(1, n_z)]
    peers += [(flip(d, k, n_doc), l) for k in range(1, n_doc)]
    for peer in peers:
        pl.semaphore_signal(barrier, inc=1, device_id=peer, device_id_type=MESH)

    own = c * n_z + z
    docs[d, own, :, 0:width] = doc_ref[...]
    short = short_ref[...]
    slots = short.shape[1]
    lane = lax.broadcasted_iota(jnp.int32, (rows, INFO), 1)
    short_wide = jnp.concatenate([short, jnp.zeros((rows, INFO - slots), jnp.int32)], axis=1)
    wide = short_wide
    for p in range(pos_n):
        at = pos_ref[:, p : p + 1]
        slot = lax.div(at, CLS)
        cluster = jnp.sum(jnp.where(lane == slot, short_wide, 0), axis=1, keepdims=True)
        wide = jnp.where(lane == slots + p, cluster, wide)
        wide = jnp.where(lane == slots + pos_n + p, lax.rem(at, CLS), wide)
    docs[d, own, :, width:] = wide.astype(F32).astype(BF16)

    pl.semaphore_wait(barrier, len(peers))

    sends = []

    def send(ref, sem, rsem, peer):
        copy = pltpu.make_async_remote_copy(
            src_ref=ref, dst_ref=ref, send_sem=sem, recv_sem=rsem, device_id=peer, device_id_type=MESH
        )
        copy.start()
        sends.append(copy)

    def arrive(ref, rsem):
        pltpu.make_async_remote_copy(
            src_ref=ref, dst_ref=ref, send_sem=cls_sem, recv_sem=rsem, device_id=(d, sib), device_id_type=MESH
        ).wait_recv()

    def slot_send(g, s, sem, peer):
        send(docs.at[g, s], sem, recv.at[g, s], peer)

    def slot_arrive(g, s):
        arrive(docs.at[g, s], recv.at[g, s])

    def same(k):
        return c * n_z + flip(z, k, n_z)

    def other(k):
        return (1 - c) * n_z + flip(z, k, n_z)

    owner = lax.div(l * here, per)
    for k in range(1, n_doc):
        to = flip(d, k, n_doc)
        copy = pltpu.make_async_remote_copy(
            src_ref=cent_ref, dst_ref=cent_in, send_sem=cent_send.at[k], recv_sem=cent_recv,
            device_id=(to, l), device_id_type=MESH,
        )

        @pl.when(d == owner)
        def _():
            copy.start()

    @pl.when(d == owner)
    def _():
        cent_in[...] = cent_ref[...]

    for k in range(n_z - 1, 0, -1):
        slot_send(d, own, z_send.at[k], (d, flip(z, k, n_z) * 2 + c))

    ring = n_doc == 4
    nears = (1, 2) if ring else tuple(range(1, n_doc))
    g_pass = flip(d, 1, n_doc) * (1 - c) + flip(d, 2, n_doc) * c
    g_keep = flip(d, 2, n_doc) * (1 - c) + flip(d, 1, n_doc) * c

    def spread(k):
        for i in nears:
            slot_send(d, same(k), g_send.at[i, k], (flip(d, i, n_doc), l))
        slot_send(d, same(k), sib_send.at[0, k], (d, sib))

    def relay(k):
        if ring:
            slot_arrive(g_pass, same(k))
            slot_send(g_pass, same(k), g_send.at[3, k], (g_keep, l))
            slot_send(g_pass, same(k), sib_send.at[1, k], (d, sib))
            slot_arrive(g_keep, same(k))
            slot_send(g_keep, same(k), sib_send.at[2, k], (d, sib))
        else:
            for i in nears:
                g = flip(d, i, n_doc)
                slot_arrive(g, same(k))
                slot_send(g, same(k), sib_send.at[i, k], (d, sib))

    ready = [d]
    for k in range(n_z):
        if k:
            slot_arrive(d, same(k))
        spread(k)
        if k:
            relay(k - 1)

    load.wait()

    def rows_of(g):
        return docs[g].reshape(group, width + INFO)

    def work(g, first, last):
        info_t[...] = rows_of(g)[:, width:].astype(F32).T
        if first:
            part[...] = jnp.zeros_like(part)

        def tile(t, carry):
            at = pl.ds(pl.multiple_of(t * TILE, TILE), TILE)
            x = rows_of(g)[:, :width]
            w = cls[at, :]
            logits = lax.dot_general(w, x, NT, preferred_element_type=F32)
            label = lax.broadcasted_iota(jnp.int32, (CLS, group), 0).astype(F32)
            pieces = []
            for j in range(TILE // CLS):
                cid = (l * here + t * (TILE // CLS) + j).astype(F32)
                member = jnp.max(jnp.where(info_t[0:slots, :] == cid, 1.0, 0.0), axis=0, keepdims=True)
                hit = None
                for p in range(pos_n):
                    pc = info_t[slots + p : slots + p + 1, :]
                    pw = info_t[slots + pos_n + p : slots + pos_n + p + 1, :]
                    this = label == jnp.where(pc == cid, pw, -1.0)
                    hit = this if hit is None else hit | this
                grad = sigmoid_grad(logits[j * CLS : (j + 1) * CLS, :], hit) * member
                pieces.append(grad.astype(BF16))
            grad = jnp.concatenate(pieces, axis=0)
            total = jnp.dot(grad, x, preferred_element_type=F32)
            if not first:
                total = total + acc[at, :]
            if last:
                gcls_ref[at, :] = total.astype(BF16)
            else:
                acc[at, :] = total
            if first:
                part[...] += lax.dot_general(grad, w, TN, preferred_element_type=F32)
            return carry

        lax.fori_loop(0, labels // TILE, tile, 0)

        def meta(cents, base):
            x = rows_of(g)[:, :width]
            logits = lax.dot_general(cents, x, NT, preferred_element_type=F32)
            cid = (lax.broadcasted_iota(jnp.int32, (per, group), 0) + base).astype(F32)
            hit = None
            for p in range(pos_n):
                this = cid == info_t[slots + p : slots + p + 1, :]
                hit = this if hit is None else hit | this
            return sigmoid_grad(logits, hit), cid

        mine, _ = meta(cent_ref[...], d * per)
        total = jnp.dot(mine.astype(BF16), rows_of(g)[:, :width], preferred_element_type=F32)
        gcent_ref[...] = total if first else gcent_ref[...] + total
        if first:
            @pl.when(d != owner)
            def _():
                arrive(cent_in, cent_recv)

            base = owner * per
            some, cid = meta(cent_in[...], base)
            low = (l * here).astype(F32)
            some = jnp.where((cid >= low) & (cid < low + here), some, 0.0).astype(BF16)
            part[...] += lax.dot_general(some, cent_in[...], TN, preferred_element_type=F32)

    for k in range(n_z):
        slot_arrive(d, other(k))
    work(d, True, n_doc == 1)

    half = group // 2
    pair_out[...] = part[pl.ds(pl.multiple_of((1 - c) * half, half), half), :].astype(BF16)
    pair = pltpu.make_async_remote_copy(
        src_ref=pair_out, dst_ref=pair_in, send_sem=pair_send, recv_sem=pair_recv,
        device_id=(d, sib), device_id_type=MESH,
    )
    pair.start()
    sends.append(pair)
    relay(n_z - 1)
    pair.wait_recv()
    tot[...] = part[pl.ds(pl.multiple_of(c * half, half), half), :] + pair_in[...].astype(F32)
    rs_out[...] = tot[...].astype(BF16).reshape(n_z, rows, width)
    for k in range(n_z - 1, 0, -1):
        to = flip(z, k, n_z)
        copy = pltpu.make_async_remote_copy(
            src_ref=rs_out.at[to], dst_ref=rs_in.at[z], send_sem=rs_send.at[k], recv_sem=rs_recv.at[z],
            device_id=(d, to * 2 + c), device_id_type=MESH,
        )
        copy.start()
        sends.append(copy)

    for i in range(1, n_doc):
        if ring:
            g = (None, g_pass, g_keep, flip(d, 3, n_doc))[i]
        else:
            g = flip(d, i, n_doc)
        for k in range(n_z):
            if ring and i == 3:
                slot_arrive(g, same(k))
                slot_send(g, same(k), sib_send.at[3, k], (d, sib))
        for k in range(n_z):
            slot_arrive(g, other(k))
        work(g, False, i == n_doc - 1)

    out = tot[pl.ds(pl.multiple_of(z * rows, rows), rows), :]
    for k in range(1, n_z):
        src = flip(z, k, n_z)
        arrive(rs_in.at[src], rs_recv.at[src])
        out = out + rs_in[src].astype(F32)
    gdoc_ref[...] = out.astype(BF16)

    for copy in sends:
        copy.wait_send()
    for k in range(1, n_doc):
        @pl.when(d == owner)
        def _():
            pltpu.make_async_remote_copy(
                src_ref=cent_ref, dst_ref=cent_in, send_sem=cent_send.at[k], recv_sem=cent_recv,
                device_id=(d, sib), device_id_type=MESH,
            ).wait_send()


def solution(mesh):
    n_doc, n_label = mesh.shape["doc"], mesh.shape["label"]
    n_z = n_label // 2

    def body(doc_embed, classifier, centroids, shortlist, positives):
        rows, width = doc_embed.shape
        labels = classifier.shape[0]
        per = centroids.shape[0]
        group = n_label * rows
        vmem = pl.BlockSpec(memory_space=pltpu.VMEM)
        dma = pltpu.SemaphoreType.DMA
        return pl.pallas_call(
            functools.partial(kernel, n_doc, n_label, positives.shape[1]),
            out_shape=(
                jax.ShapeDtypeStruct((labels, width), BF16),
                jax.ShapeDtypeStruct((per, width), F32),
                jax.ShapeDtypeStruct((rows, width), BF16),
            ),
            in_specs=[vmem, pl.BlockSpec(memory_space=pl.ANY), vmem, vmem, vmem],
            out_specs=(vmem, vmem, vmem),
            scratch_shapes=[
                pltpu.VMEM((n_doc, n_label, rows, width + INFO), BF16),
                pltpu.VMEM((labels, width), BF16),
                pltpu.VMEM((INFO, group), F32),
                pltpu.VMEM((labels, width), F32),
                pltpu.VMEM((group, width), F32),
                pltpu.VMEM((per, width), BF16),
                pltpu.VMEM((group // 2, width), BF16),
                pltpu.VMEM((group // 2, width), BF16),
                pltpu.VMEM((group // 2, width), F32),
                pltpu.VMEM((n_z, rows, width), BF16),
                pltpu.VMEM((n_z, rows, width), BF16),
                dma(()),
                dma((n_doc, n_z)),
                dma((n_z,)),
                dma((n_doc, n_z)),
                dma((n_doc,)),
                dma(()),
                dma((n_z,)),
                dma((n_doc, n_label)),
                dma(()),
                dma(()),
                dma((n_z,)),
            ],
            compiler_params=pltpu.CompilerParams(
                collective_id=0, has_side_effects=True, vmem_limit_bytes=60 * 1024 * 1024
            ),
        )(doc_embed, classifier, centroids, shortlist, positives)

    in_specs = (
        P(("doc", "label"), None),
        P("label", None),
        P("doc", None),
        P(("doc", "label"), None),
        P(("doc", "label"), None),
    )
    out_specs = (P("label", None), P("doc", None), P(("doc", "label"), None))
    return jax.shard_map(body, mesh=mesh, in_specs=in_specs, out_specs=out_specs, check_vma=False)
```

```python
import functools

import jax
import jax.numpy as jnp
from jax import lax
from jax.experimental import pallas as pl
from jax.experimental.pallas import tpu as pltpu
from jax.sharding import PartitionSpec as P

CLS = 128
INFO = 128
EIGHTH = 0.125
F32 = jnp.float32
BF16 = jnp.bfloat16
MESH = pl.DeviceIdType.MESH
NT = (((1,), (1,)), ((), ()))
TN = (((0,), (0,)), ((), ()))


def flip(a, k, n):
    out, bit = 0, 1
    while bit < n:
        b = lax.rem(lax.div(a, bit), 2)
        out = out + bit * ((1 - b) if (k // bit) % 2 else b)
        bit *= 2
    return out


def sigmoid_grad(logits, target):
    return (EIGHTH / 2) * jnp.tanh(0.5 * logits) + jnp.where(target, -EIGHTH / 2, EIGHTH / 2)


def kernel(
    n_doc, n_label, pos_n,
    doc_ref, cls_hbm, cent_ref, short_ref, pos_ref,
    gcls_ref, gcent_ref, gdoc_ref,
    docs, cls, info_t, acc, part, cent_in, pair_out, pair_in, tot, rs_out, rs_in,
    cls_sem, sib_send, z_send, g_send, cent_send, pair_send, rs_send,
    sib_recv, z_recv, g_recv, cent_recv, pair_recv, rs_recv,
):
    rows, width = doc_ref.shape
    labels = cls.shape[0]
    here = labels // CLS
    per = cent_ref.shape[0]
    n_z = n_label // 2
    group = n_label * rows
    step = min(labels, max(2 * CLS, (1 << 18) // group))
    d = lax.axis_index("doc")
    l = lax.axis_index("label")
    z, c = lax.div(l, 2), lax.rem(l, 2)
    sib = z * 2 + (1 - c)

    load = pltpu.make_async_copy(cls_hbm, cls, cls_sem)
    load.start()

    barrier = pltpu.get_barrier_semaphore()
    peers = [(d, sib)]
    peers += [(d, flip(z, k, n_z) * 2 + c) for k in range(1, n_z)]
    peers += [(flip(d, k, n_doc), l) for k in range(1, n_doc)]
    for peer in peers:
        pl.semaphore_signal(barrier, inc=1, device_id=peer, device_id_type=MESH)

    docs[0, 0, 0, :, 0:width] = doc_ref[...]
    short = short_ref[...]
    slots = short.shape[1]
    lane = lax.broadcasted_iota(jnp.int32, (rows, INFO), 1)
    short_wide = jnp.concatenate([short, jnp.zeros((rows, INFO - slots), jnp.int32)], axis=1)
    pos_t = pos_ref[...].T
    wide = short_wide
    for p in range(pos_n):
        at = pos_t[:, p : p + 1]
        slot = lax.div(at, CLS)
        cluster = jnp.sum(jnp.where(lane == slot, short_wide, 0), axis=1, keepdims=True)
        wide = jnp.where(lane == slots + p, cluster, wide)
        wide = jnp.where(lane == slots + pos_n + p, lax.rem(at, CLS), wide)
    docs[0, 0, 0, :, width:] = wide.astype(F32).astype(BF16)

    pl.semaphore_wait(barrier, len(peers))

    sends = []

    def send(src, dst, sem, rsem, peer):
        copy = pltpu.make_async_remote_copy(
            src_ref=src, dst_ref=dst, send_sem=sem, recv_sem=rsem, device_id=peer, device_id_type=MESH
        )
        copy.start()
        sends.append(copy)

    def arrive(ref, rsem):
        pltpu.make_async_remote_copy(
            src_ref=ref, dst_ref=ref, send_sem=cls_sem, recv_sem=rsem, device_id=(d, sib), device_id_type=MESH
        ).wait_recv()

    parts = (pl.ds(0, 1), pl.ds(1, n_z - 1))

    def across(h):
        for i in range(1, n_doc):
            send(docs.at[0, 0, parts[h]], docs.at[i, 0, parts[h]], g_send.at[i, h], g_recv.at[i, h], (flip(d, i, n_doc), l))

    def to_sibling(i):
        send(docs.at[i, 0], docs.at[i, 1], sib_send.at[i], sib_recv.at[i], (d, sib))

    owner = lax.div(l * here, per)
    for k in range(1, n_doc):
        to = flip(d, k, n_doc)
        copy = pltpu.make_async_remote_copy(
            src_ref=cent_ref, dst_ref=cent_in, send_sem=cent_send.at[k], recv_sem=cent_recv,
            device_id=(to, l), device_id_type=MESH,
        )

        @pl.when(d == owner)
        def _():
            copy.start()

    @pl.when(d == owner)
    def _():
        cent_in[...] = cent_ref[...]

    for k in range(n_z - 1, 0, -1):
        send(docs.at[0, 0, 0], docs.at[0, 0, k], z_send.at[k], z_recv.at[k], (d, flip(z, k, n_z) * 2 + c))
    across(0)
    for k in range(1, n_z):
        arrive(docs.at[0, 0, k], z_recv.at[k])
    to_sibling(0)
    across(1)

    load.wait()

    def rows_of(g):
        return docs[g].reshape(group, width + INFO)

    def work(g, first, last):
        info_t[...] = rows_of(g)[:, width:].astype(F32).T
        if first:
            part[...] = jnp.zeros_like(part)

        def tile(t, carry):
            at = pl.ds(pl.multiple_of(t * step, step), step)
            x = rows_of(g)[:, :width]
            w = cls[at, :]
            logits = lax.dot_general(w, x, NT, preferred_element_type=F32)
            label = lax.broadcasted_iota(jnp.int32, (CLS, group), 0).astype(F32)
            pieces = []
            for j in range(step // CLS):
                cid = (l * here + t * (step // CLS) + j).astype(F32)
                member = jnp.max(jnp.where(info_t[0:slots, :] == cid, 1.0, 0.0), axis=0, keepdims=True)
                hit = None
                for p in range(pos_n):
                    pc = info_t[slots + p : slots + p + 1, :]
                    pw = info_t[slots + pos_n + p : slots + pos_n + p + 1, :]
                    this = label == jnp.where(pc == cid, pw, -1.0)
                    hit = this if hit is None else hit | this
                grad = sigmoid_grad(logits[j * CLS : (j + 1) * CLS, :], hit) * member
                pieces.append(grad.astype(BF16))
            grad = jnp.concatenate(pieces, axis=0)
            total = jnp.dot(grad, x, preferred_element_type=F32)
            if not first:
                total = total + acc[at, :]
            if last:
                gcls_ref[at, :] = total.astype(BF16)
            else:
                acc[at, :] = total
            if first:
                part[...] += lax.dot_general(grad, w, TN, preferred_element_type=F32)
            return carry

        lax.fori_loop(0, labels // step, tile, 0)

        def meta(cents, base):
            x = rows_of(g)[:, :width]
            logits = lax.dot_general(cents, x, NT, preferred_element_type=F32)
            cid = (lax.broadcasted_iota(jnp.int32, (per, group), 0) + base).astype(F32)
            hit = None
            for p in range(pos_n):
                this = cid == info_t[slots + p : slots + p + 1, :]
                hit = this if hit is None else hit | this
            return sigmoid_grad(logits, hit), cid

        mine, _ = meta(cent_ref[...], d * per)
        total = jnp.dot(mine.astype(BF16), rows_of(g)[:, :width], preferred_element_type=F32)
        gcent_ref[...] = total if first else gcent_ref[...] + total
        if first:
            @pl.when(d != owner)
            def _():
                arrive(cent_in, cent_recv)

            base = owner * per
            some, cid = meta(cent_in[...], base)
            low = (l * here).astype(F32)
            some = jnp.where((cid >= low) & (cid < low + here), some, 0.0).astype(BF16)
            part[...] += lax.dot_general(some, cent_in[...], TN, preferred_element_type=F32)

    arrive(docs.at[0, 1], sib_recv.at[0])
    work(0, True, n_doc == 1)

    half = group // 2
    pair_out[...] = part[half:, :].astype(BF16)
    send(pair_out, pair_in, pair_send, pair_recv, (d, sib))
    for i in range(1, n_doc):
        for h in range(2):
            arrive(docs.at[i, 0, parts[h]], g_recv.at[i, h])
        to_sibling(i)
    arrive(pair_in, pair_recv)
    tot[...] = part[:half, :] + pair_in[...].astype(F32)
    rs_out[...] = tot[...].astype(BF16).reshape(n_z, rows, width)
    for k in range(n_z - 1, 0, -1):
        send(rs_out.at[k], rs_in.at[k], rs_send.at[k], rs_recv.at[k], (d, flip(z, k, n_z) * 2 + c))

    for i in range(1, n_doc):
        arrive(docs.at[i, 1], sib_recv.at[i])
        work(i, False, i == n_doc - 1)

    out = tot[0:rows, :]
    for k in range(1, n_z):
        arrive(rs_in.at[k], rs_recv.at[k])
        out = out + rs_in[k].astype(F32)
    gdoc_ref[...] = out.astype(BF16)

    for copy in sends:
        copy.wait_send()
    for k in range(1, n_doc):
        @pl.when(d == owner)
        def _():
            pltpu.make_async_remote_copy(
                src_ref=cent_ref, dst_ref=cent_in, send_sem=cent_send.at[k], recv_sem=cent_recv,
                device_id=(d, sib), device_id_type=MESH,
            ).wait_send()


def settle_kernel(n, *refs):
    copies = [pltpu.make_async_copy(refs[i], refs[n + i], refs[2 * n].at[i]) for i in range(n)]
    for copy in copies:
        copy.start()
    for copy in copies:
        copy.wait()


def settle(*arrays):
    n = len(arrays)
    return pl.pallas_call(
        functools.partial(settle_kernel, n),
        out_shape=tuple(jax.ShapeDtypeStruct(a.shape, a.dtype) for a in arrays),
        in_specs=[pl.BlockSpec(memory_space=pl.ANY)] * n,
        out_specs=(pl.BlockSpec(memory_space=pl.ANY),) * n,
        scratch_shapes=[pltpu.SemaphoreType.DMA((n,))],
        compiler_params=pltpu.CompilerParams(vmem_limit_bytes=1 << 20),
    )(*arrays)


def solution(mesh):
    n_doc, n_label = mesh.shape["doc"], mesh.shape["label"]
    n_z = n_label // 2

    def body(doc_embed, classifier, centroids, shortlist, positives):
        rows, width = doc_embed.shape
        labels = classifier.shape[0]
        per = centroids.shape[0]
        group = n_label * rows
        vmem = pl.BlockSpec(memory_space=pltpu.VMEM)
        limit = (64 << 20) - (labels * width * 2 + per * width * 4 + rows * width * 2) - (128 << 10)
        dma = pltpu.SemaphoreType.DMA
        outs = pl.pallas_call(
            functools.partial(kernel, n_doc, n_label, positives.shape[1]),
            out_shape=(
                pltpu.VMEM((labels, width), BF16),
                pltpu.VMEM((per, width), F32),
                pltpu.VMEM((rows, width), BF16),
            ),
            in_specs=[vmem, pl.BlockSpec(memory_space=pl.ANY), vmem, vmem, vmem],
            out_specs=(vmem, vmem, vmem),
            scratch_shapes=[
                pltpu.VMEM((n_doc, 2, n_z, rows, width + INFO), BF16),
                pltpu.VMEM((labels, width), BF16),
                pltpu.VMEM((INFO, group), F32),
                pltpu.VMEM((labels, width), F32),
                pltpu.VMEM((group, width), F32),
                pltpu.VMEM((per, width), BF16),
                pltpu.VMEM((group // 2, width), BF16),
                pltpu.VMEM((group // 2, width), BF16),
                pltpu.VMEM((group // 2, width), F32),
                pltpu.VMEM((n_z, rows, width), BF16),
                pltpu.VMEM((n_z, rows, width), BF16),
                dma(()),
                dma((n_doc,)),
                dma((n_z,)),
                dma((n_doc, 2)),
                dma((n_doc,)),
                dma(()),
                dma((n_z,)),
                dma((n_doc,)),
                dma((n_z,)),
                dma((n_doc, 2)),
                dma(()),
                dma(()),
                dma((n_z,)),
            ],
            compiler_params=pltpu.CompilerParams(
                collective_id=0, has_side_effects=True, vmem_limit_bytes=limit
            ),
        )(doc_embed, classifier, centroids, shortlist, positives.T)
        return settle(*outs)

    in_specs = (
        P(("doc", "label"), None),
        P("label", None),
        P("doc", None),
        P(("doc", "label"), None),
        P(("doc", "label"), None),
    )
    out_specs = (P("label", None), P("doc", None), P(("doc", "label"), None))
    return jax.shard_map(body, mesh=mesh, in_specs=in_specs, out_specs=out_specs, check_vma=False)
```
